32 devices in a mesh: dp: 4 (over y, x), latent: 8 (over z, core).
Axes of the slice: x: 2, y: 2, z: 4, core: 2. Of those that a mesh axis runs over, the one named last changes fastest.
Arguments:
- paired: bfloat16 [1024, 8192], P('dp'), may hold values from -6 to 6
- enc_weight: float32 [8192, 8192], P('dp', 'latent'), may hold values from -0.0625 to 0.0625
- enc_bias: float32 [8192], P('latent'), may hold values from -3 to 3
- dec_weight: float32 [8192, 8192], P('latent', 'dp'), may hold values from -0.21931359 to 0.21931359
- dec_bias: float32 [8192], P('dp'), may hold values from -3 to 3
- buffer_rows: bfloat16 [4096, 8192], P('dp', 'latent'), may hold values from -6 to 6
- block_dest: int32 [64], replicated, may hold values from 0 to 63, as said below
Outputs:
- enc_grad: float32 [8192, 8192], P('dp', 'latent')
- dec_grad: float32 [8192, 8192], P('latent', 'dp')
- shuffled: bfloat16 [4096, 8192], P('dp', 'latent')
The draws below stay inside these ranges and needn't reach their ends.
Inputs may be any that keep to these rules, and one draw needn't show every extreme that they name: `block_dest`: a permutation of the 64 blocks; the 16 blocks of each index of dp go exactly 4 to each index of dp.
All inputs are finite; a program needn't handle non-finite values.
Results may differ from the reference program's by a relative error of at most 0.014.
Values may be sent and summed in bfloat16 or wider, within the bound.
A program may use at most 192 MiB of HBM per device.

```python
import jax
import jax.numpy as jnp
from jax import lax

D = 4096
LATENTS = 8192
BLOCK_ROWS = 64
TOKENS = 1024
BUF = 4096
NBLK_DEV = 16
BLOCKS = 64
N_DP = 4
N_LATENT = 8


def draw_dec_weight(key, part):
    key = jax.random.fold_in(key, 11)
    base_key, row_key = jax.random.split(key)
    position = (jnp.arange(2 * D) % D).astype(jnp.float32) / D
    base = jnp.clip(jax.random.normal(base_key, (LATENTS, 2 * D), jnp.float32), -4.0, 4.0)
    column_scale = jnp.exp(position * jnp.log(10.0)) * 0.049606
    row_scale = jnp.exp(jax.random.uniform(row_key, (LATENTS, 1), jnp.float32) * jnp.log(10.0))
    return base * row_scale * column_scale[None, :] / jnp.sqrt(jnp.float32(LATENTS))


def draw_block_dest(key, part):
    key = jax.random.fold_in(key, 5)
    owner_key, local_key = jax.random.split(key)
    device_total = BLOCKS // NBLK_DEV
    labels = jnp.arange(NBLK_DEV, dtype=jnp.int32) % device_total
    sender_of = jax.vmap(lambda k: jax.random.permutation(k, labels))(jax.random.split(owner_key, device_total)).reshape(-1)
    onehot = (sender_of[:, None] == jnp.arange(device_total, dtype=jnp.int32)[None, :]).astype(jnp.int32)
    sender_rank = jnp.sum((jnp.cumsum(onehot, axis=0) - onehot) * onehot, axis=1)
    local_order = jax.vmap(lambda k: jax.random.permutation(k, NBLK_DEV))(jax.random.split(local_key, device_total)).astype(jnp.int32)
    source_block = sender_of * NBLK_DEV + local_order[sender_of, sender_rank]
    return jnp.zeros((BLOCKS,), jnp.int32).at[source_block].set(jnp.arange(BLOCKS, dtype=jnp.int32))


def block_scale(stream_key, dims, pieces, least, largest):
    def one(dim, blocks):
        steps = jax.random.uniform(jax.random.fold_in(jax.random.fold_in(stream_key, 6), dim), (blocks,), jnp.float32, least / len(pieces), largest / len(pieces))
        return jnp.repeat(jnp.exp(steps), dims[dim] // blocks).reshape((-1,) + (1,) * (len(dims) - dim - 1))

    gain = one(*pieces[0])
    for cut in pieces[1:]:
        gain = gain * one(*cut)
    return gain


def normal_values(rng, extent, deviation, reach, pieces=(), kind=jnp.bfloat16):
    loudness = block_scale(rng, extent, pieces, -0.22, 0.18) if pieces else 1.0
    entries = jax.random.normal(rng, extent, jnp.float32) * deviation * loudness
    return jnp.minimum(jnp.maximum(entries, -reach), reach).astype(kind)


def setup_inputs(seed: int = 0) -> dict:
    seeds = jax.random.split(jax.random.key(seed), 8)
    return {
        "paired": normal_values(seeds[0], (TOKENS, 2 * D), 1.0, 6.0, ((0, 4),)),
        "enc_weight": normal_values(seeds[1], (2 * D, LATENTS), (2 * D) ** -0.5, 0.0625, ((0, 4), (1, 8)), jnp.float32),
        "enc_bias": normal_values(seeds[2], (LATENTS,), 0.5, 3.0, ((0, 8),), jnp.float32),
        "dec_weight": draw_dec_weight(jax.random.fold_in(seeds[7], 71), 0),
        "dec_bias": normal_values(seeds[4], (2 * D,), 0.5, 3.0, ((0, 4),), jnp.float32),
        "buffer_rows": normal_values(seeds[5], (BUF, 2 * D), 1.0, 6.0, ((0, 4), (1, 8))),
        "block_dest": draw_block_dest(jax.random.fold_in(seeds[7], 71), 0),
    }


loss_scale = 0.03125
sparsity_weight = 4.0
norm_eps = 1e-06

def reference(paired, enc_weight, enc_bias, dec_weight, dec_bias, buffer_rows, block_dest):
    width = 2 * D
    lat_group = LATENTS // N_LATENT
    feat_group = width // N_DP
    enc16 = enc_weight.astype(jnp.bfloat16)
    dec16 = dec_weight.astype(jnp.bfloat16)
    preact = jnp.dot(paired, enc16, preferred_element_type=jnp.float32) + enc_bias
    activated = jnp.maximum(preact, 0.0)
    latent_codes = (activated * activated).astype(jnp.bfloat16)
    code_groups = latent_codes.reshape(TOKENS, N_LATENT, lat_group).transpose(1, 0, 2)
    dec_groups = dec16.reshape(N_LATENT, lat_group, width)

    def add_recon(running, pair):
        code_block, dec_block = pair
        partial_sum = jnp.dot(code_block, dec_block, preferred_element_type=jnp.float32)
        rounded = lax.optimization_barrier(partial_sum.astype(jnp.bfloat16))
        return (running + rounded.astype(jnp.float32), None)
    recon, _ = lax.scan(add_recon, jnp.zeros((TOKENS, width), jnp.float32), (code_groups, dec_groups))
    recon = recon + dec_bias
    recon_error = recon - paired.astype(jnp.float32)
    split_weight = dec_weight.reshape(LATENTS, 2, D)
    dec_norms = jnp.sqrt(lax.optimization_barrier(jnp.sum(split_weight * split_weight, axis=2)) + norm_eps)
    error_grad = (2.0 * loss_scale * recon_error).astype(jnp.bfloat16)
    code_sum = lax.optimization_barrier(jnp.sum(latent_codes.astype(jnp.float32), axis=0))
    dec_main = jnp.dot(latent_codes.T, error_grad, preferred_element_type=jnp.float32)
    sparse_part = sparsity_weight * loss_scale * code_sum[:, None, None] * split_weight / dec_norms[:, :, None]
    dec_grad = dec_main + sparse_part.reshape(LATENTS, width)
    error_groups = error_grad.reshape(TOKENS, N_DP, feat_group).transpose(1, 0, 2)
    dec_col_groups = dec16.reshape(LATENTS, N_DP, feat_group).transpose(1, 0, 2)

    def add_code(running, pair):
        error_block, dec_block = pair
        partial_sum = jnp.dot(error_block, dec_block.T, preferred_element_type=jnp.float32)
        rounded = lax.optimization_barrier(partial_sum.astype(jnp.bfloat16))
        return (running + rounded.astype(jnp.float32), None)
    code_grad, _ = lax.scan(add_code, jnp.zeros((TOKENS, LATENTS), jnp.float32), (error_groups, dec_col_groups))
    code_grad = code_grad + sparsity_weight * loss_scale * (dec_norms[:, 0] + dec_norms[:, 1])
    preact_grad = (code_grad * 2.0 * activated).astype(jnp.bfloat16)
    enc_grad = jnp.dot(paired.T, preact_grad, preferred_element_type=jnp.float32)
    source_block = jnp.zeros((BLOCKS,), jnp.int32).at[block_dest].set(jnp.arange(BLOCKS, dtype=jnp.int32))
    blocks_all = buffer_rows.reshape(BLOCKS, BLOCK_ROWS, width)
    shuffled = blocks_all[source_block].reshape(BUF, width)
    return (enc_grad, dec_grad, shuffled)
```

```python
import jax
import jax.numpy as jnp
from jax import lax
from jax.sharding import PartitionSpec as P

BLOCK_ROWS = 64


loss_scale = 0.03125
sparsity_weight = 4.0
norm_eps = 1e-06


def body(paired, enc_weight, enc_bias, dec_weight, dec_bias, buffer_rows, block_dest):
    data_count = lax.axis_size("dp")
    latent_count = lax.axis_size("latent")
    data_index = lax.axis_index("dp")
    latent_index = lax.axis_index("latent")
    own_rows = paired.shape[0]
    total_rows = own_rows * data_count
    error_count = total_rows // latent_count
    enc16 = enc_weight.astype(jnp.bfloat16)
    dec16 = dec_weight.astype(jnp.bfloat16)
    contract_rows = (((0,), (0,)), ((), ()))
    contract_cols = (((1,), (1,)), ((), ()))
    column_rows = lax.all_to_all(paired, "dp", split_axis=1, concat_axis=0, tiled=True)
    preact = lax.psum_scatter(
        jnp.dot(column_rows, enc16, preferred_element_type=jnp.float32).astype(jnp.bfloat16),
        "dp",
        scatter_dimension=0,
        tiled=True,
    ).astype(jnp.float32)
    preact = preact + enc_bias
    activated = jnp.maximum(preact, 0.0)
    latent_codes = (activated * activated).astype(jnp.bfloat16)
    all_codes = lax.all_gather(latent_codes, "dp", axis=0, tiled=True)
    row_block = all_codes
    recon = (
        lax.psum_scatter(
            jnp.dot(row_block, dec16, preferred_element_type=jnp.float32).astype(jnp.bfloat16),
            "latent",
            scatter_dimension=0,
            tiled=True,
        ).astype(jnp.float32)
        + dec_bias
    )
    target_rows = lax.dynamic_slice_in_dim(column_rows, latent_index * error_count, error_count, 0)
    recon_error = recon - target_rows.astype(jnp.float32)
    half_count = data_count // 2
    model_index = data_index // half_count
    local_squares = jnp.sum(dec_weight * dec_weight, axis=1)
    square_pair = jnp.stack(
        [
            jnp.where(model_index == 0, local_squares, 0.0),
            jnp.where(model_index == 1, local_squares, 0.0),
        ]
    )
    square_sums = lax.psum(square_pair, "dp")
    dec_norms = jnp.sqrt(square_sums + norm_eps)
    own_norm = jnp.where(model_index == 0, dec_norms[0], dec_norms[1])
    error_grad = (2.0 * loss_scale * recon_error).astype(jnp.bfloat16)
    all_errors = lax.all_gather(error_grad, "latent", axis=0, tiled=True)
    code_sum = jnp.sum(all_codes, axis=0, dtype=jnp.float32)
    dec_main = lax.dot_general(
        all_codes, all_errors, contract_rows, preferred_element_type=jnp.float32
    )
    dec_grad = (
        dec_main + sparsity_weight * loss_scale * code_sum[:, None] * dec_weight / own_norm[:, None]
    )
    row_block = all_errors
    code_grad = lax.psum_scatter(
        lax.dot_general(row_block, dec16, contract_cols, preferred_element_type=jnp.float32).astype(
            jnp.bfloat16
        ),
        "dp",
        scatter_dimension=0,
        tiled=True,
    ).astype(jnp.float32)
    code_grad = code_grad + sparsity_weight * loss_scale * (dec_norms[0] + dec_norms[1])
    preact_grad = (code_grad * 2.0 * activated).astype(jnp.bfloat16)
    all_preact_grads = lax.all_gather(preact_grad, "dp", axis=0, tiled=True)
    enc_grad = lax.dot_general(
        column_rows, all_preact_grads, contract_rows, preferred_element_type=jnp.float32
    )
    blocks_here = buffer_rows.shape[0] // BLOCK_ROWS
    per_device = blocks_here // data_count
    block_iota = jnp.arange(blocks_here, dtype=jnp.int32)
    own_dest = lax.dynamic_slice_in_dim(block_dest, data_index * blocks_here, blocks_here, 0)
    target_device = own_dest // blocks_here
    earlier_same = (target_device[None, :] == target_device[:, None]) & (
        own_dest[None, :] < own_dest[:, None]
    )
    send_slot = target_device * per_device + jnp.sum(earlier_same.astype(jnp.int32), axis=1)
    chosen = jnp.sum(
        jnp.where(send_slot[None, :] == block_iota[:, None], block_iota[None, :], 0), axis=1
    )
    feature_count = buffer_rows.shape[1]
    outgoing = buffer_rows.reshape(blocks_here, BLOCK_ROWS, feature_count)[chosen].reshape(
        buffer_rows.shape
    )
    arrived = lax.all_to_all(outgoing, "dp", split_axis=0, concat_axis=0, tiled=True)
    positions = data_index * blocks_here + block_iota
    every_block = jnp.arange(block_dest.shape[0], dtype=jnp.int32)
    source_block = jnp.sum(
        jnp.where(block_dest[None, :] == positions[:, None], every_block[None, :], 0), axis=1
    )
    sender_device = source_block // blocks_here
    before_same = (sender_device[None, :] == sender_device[:, None]) & (
        block_iota[None, :] < block_iota[:, None]
    )
    arrival_slot = sender_device * per_device + jnp.sum(before_same.astype(jnp.int32), axis=1)
    shuffled = arrived.reshape(blocks_here, BLOCK_ROWS, feature_count)[arrival_slot].reshape(
        buffer_rows.shape
    )
    return (enc_grad, dec_grad, shuffled)


def solution(mesh):
    in_specs = (
        P("dp", None),
        P("dp", "latent"),
        P("latent"),
        P("latent", "dp"),
        P("dp"),
        P("dp", "latent"),
        P(),
    )
    out_specs = (P("dp", "latent"), P("latent", "dp"), P("dp", "latent"))
    return jax.shard_map(body, mesh=mesh, in_specs=in_specs, out_specs=out_specs, check_vma=False)
```

```python
import functools

import jax
import jax.numpy as jnp
from jax import lax
from jax.experimental import pallas as pl
from jax.experimental.pallas import tpu as pltpu
from jax.sharding import PartitionSpec as P

BLOCK_ROWS = 64
CHUNKS = 4
TILE = 256
MESH = pl.DeviceIdType.MESH

loss_scale = 0.03125
sparsity_weight = 4.0
norm_eps = 1e-06


def rounds_of(latent_count):
    return (latent_count // 2).bit_length() - 1


def kernel(
    nd, nl, chunks,
    paired, enc_w, dec_w, enc_b, dec_b, outgoing,
    col_out, codes_out, err_out, pg_out, norms_out, arrived,
    col, enc16, dec16, stage, part, prec, act, codes, rp, crx, zrx, err, cgp, cgr, pg, sq, sqr,
    local_sem, pair_s, pair_r, fwd_s, fwd_r, pp_s, pp_r, cd_s, cd_r, cx_s, cx_r, zx_s, zx_r,
    za_s, za_r, ca_s, ca_r, cg_s, cg_r, pg_s, pg_r, sq_s, sq_r, bf_s, bf_r, own_sem, out_sem,
):
    f32, bf16 = jnp.float32, jnp.bfloat16
    rows = paired.shape[0] // chunks
    feats, lats = enc_w.shape
    m = rows * nd
    half = feats // 2
    nb = rounds_of(nl)
    me = lax.axis_index("dp")
    li = lax.axis_index("latent")
    zi = lax.div(li, 2)
    core = lax.rem(li, 2)
    mate = {"latent": li + 1 - 2 * core}
    bits = [lax.rem(lax.div(zi, 1 << b), 2) for b in range(nb)]
    zpeer = [{"latent": li + (2 << b) * (1 - 2 * bits[b])} for b in range(nb)]
    ahead = [lax.rem(me + k, nd) for k in range(nd)]
    behind = [lax.rem(me + nd - k, nd) for k in range(nd)]
    dpeer = [{"dp": ahead[k]} for k in range(nd)]

    def at_rows(index, size):
        return pl.ds(pl.multiple_of(index, 16), size)

    my_rows = at_rows(me * rows, rows)

    def remote(src, dst, s, r, dev):
        return pltpu.make_async_remote_copy(
            src_ref=src, dst_ref=dst, send_sem=s, recv_sem=r, device_id=dev, device_id_type=MESH
        )

    enc_copy = pltpu.make_async_copy(enc_w, stage, local_sem.at[0])
    enc_copy.start()

    barrier = pltpu.get_barrier_semaphore()
    friends = dpeer[1:] + [mate] + zpeer
    for dev in friends:
        pl.semaphore_signal(barrier, inc=1, device_id=dev, device_id_type=MESH)
    pl.semaphore_wait(barrier, len(friends))

    sends = []

    def go(copy):
        copy.start()
        sends.append(copy)
        return copy

    my_half = pl.ds(pl.multiple_of(core * half, 128), half)
    pair_copies, fwd_copies, own_copies = {}, {}, {}
    for c in range(chunks):
        for k in range(1, nd):
            source = pl.ds(pl.multiple_of(ahead[k] * feats + core * half, 128), half)
            pair_copies[c, k] = go(remote(
                paired.at[pl.ds(c * rows, rows), source],
                col.at[c, my_rows, my_half],
                pair_s.at[c, k - 1], pair_r.at[c, k - 1], dpeer[k],
            ))
        own_copies[c] = pltpu.make_async_copy(
            paired.at[pl.ds(c * rows, rows), pl.ds(pl.multiple_of(me * feats, 128), feats)],
            col.at[c, my_rows],
            own_sem.at[c],
        )
        own_copies[c].start()
    own_block = pltpu.make_async_copy(outgoing.at[me], arrived.at[me], local_sem.at[2])
    own_block.start()

    enc_copy.wait()

    @pl.loop(0, feats // 128)
    def _(i):
        r = pl.ds(pl.multiple_of(i * 128, 128), 128)
        enc16[r, :] = stage[r, :].astype(bf16)

    def forward(c):
        for k in range(1, nd):
            pair_copies[c, k].wait_recv()
            block = col.at[c, at_rows(behind[k] * rows, rows), my_half]
            fwd_copies[c, k] = go(remote(block, block, fwd_s.at[c, k - 1], fwd_r.at[c, k - 1], mate))

    pp_copies, cd_copies, cx_copies, zx_copies = {}, {}, {}, {}
    za_copies, ca_copies, cg_copies, pg_copies = {}, {}, {}, {}

    def encode(c):
        own_copies[c].wait()
        for k in range(1, nd):
            fwd_copies[c, k].wait_recv()

        @pl.loop(0, lats // TILE)
        def _(j):
            t = pl.ds(pl.multiple_of(j * TILE, TILE), TILE)
            part[c, :, t] = jnp.dot(col[c], enc16[:, t], preferred_element_type=f32).astype(bf16)

        for k in range(1, nd):
            pp_copies[c, k] = go(remote(
                part.at[c, at_rows(ahead[k] * rows, rows)], prec.at[c, k - 1],
                pp_s.at[c, k - 1], pp_r.at[c, k - 1], dpeer[k],
            ))

    def activate(c):
        for k in range(1, nd):
            pp_copies[c, k].wait_recv()
        total = part[c, my_rows, :].astype(f32)
        for k in range(1, nd):
            total = total + prec[c, k - 1].astype(f32)
        a = jnp.maximum(total + enc_b[...], 0.0)
        act[c] = a
        codes[c, my_rows, :] = (a * a).astype(bf16)
        for k in range(1, nd):
            block = codes.at[c, my_rows]
            cd_copies[c, k] = go(remote(block, block, cd_s.at[c, k - 1], cd_r.at[c, k - 1], dpeer[k]))

    def decode(c):
        for k in range(1, nd):
            cd_copies[c, k].wait_recv()

        @pl.loop(0, feats // TILE)
        def _(j):
            t = pl.ds(pl.multiple_of(j * TILE, TILE), TILE)
            rp[c, :, t] = jnp.dot(codes[c], dec16[:, t], preferred_element_type=f32).astype(bf16)

        cx_copies[c] = go(remote(
            rp.at[c, at_rows((1 - core) * (m // 2), m // 2)], crx.at[c], cx_s.at[c], cx_r.at[c], mate
        ))

    bases, sizes = [core * (m // 2)], [m // 2]
    for b in range(nb):
        sizes.append(sizes[-1] // 2)
        bases.append(bases[-1] + bits[b] * sizes[-1])
    zoff = [0]
    for b in range(nb):
        zoff.append(zoff[-1] + sizes[b + 1])

    def add_rows(c, base, size, source, start):
        @pl.loop(0, size // 32)
        def _(i):
            r = at_rows(base + i * 32, 32)
            s = at_rows(start + i * 32, 32)
            rp[c, r, :] = (rp[c, r, :].astype(f32) + source[c, s, :].astype(f32)).astype(bf16)

    def halve(b, c):
        if b == 0:
            cx_copies[c].wait_recv()
            add_rows(c, bases[0], sizes[0], crx, 0)
        else:
            zx_copies[c, b - 1].wait_recv()
            add_rows(c, bases[b], sizes[b], zrx, zoff[b - 1])
        size = sizes[b + 1]
        zx_copies[c, b] = go(remote(
            rp.at[c, at_rows(bases[b] + (1 - bits[b]) * size, size)],
            zrx.at[c, pl.ds(zoff[b], size)],
            zx_s.at[c, b], zx_r.at[c, b], zpeer[b],
        ))

    def spread(b, c):
        block = err.at[c, at_rows(bases[b + 1], sizes[b + 1])]
        za_copies[c, b] = go(remote(block, block, za_s.at[c, b], za_r.at[c, b], zpeer[b]))

    def error(c):
        b = nb - 1
        zx_copies[c, b].wait_recv()

        @pl.loop(0, sizes[nb] // 32)
        def _(i):
            r = at_rows(bases[nb] + i * 32, 32)
            s = at_rows(zoff[b] + i * 32, 32)
            recon = rp[c, r, :].astype(f32) + zrx[c, s, :].astype(f32) + dec_b[...]
            err[c, r, :] = (2.0 * loss_scale * (recon - col[c, r, :].astype(f32))).astype(bf16)

        spread(b, c)

    def widen(b, c):
        za_copies[c, b + 1].wait_recv()
        spread(b, c)

    def share(c):
        za_copies[c, 0].wait_recv()
        block = err.at[c, at_rows(bases[0], m // 2)]
        ca_copies[c] = go(remote(block, block, ca_s.at[c], ca_r.at[c], mate))

    def back(c):
        ca_copies[c].wait_recv()

        @pl.loop(0, lats // TILE)
        def _(j):
            t = pl.ds(pl.multiple_of(j * TILE, TILE), TILE)
            cgp[c, :, t] = lax.dot_general(
                err[c], dec16[t, :], (((1,), (1,)), ((), ())), preferred_element_type=f32
            ).astype(bf16)

        for k in range(1, nd):
            cg_copies[c, k] = go(remote(
                cgp.at[c, at_rows(ahead[k] * rows, rows)], cgr.at[c, k - 1],
                cg_s.at[c, k - 1], cg_r.at[c, k - 1], dpeer[k],
            ))

    def grad(c):
        for k in range(1, nd):
            cg_copies[c, k].wait_recv()
        total = cgp[c, my_rows, :].astype(f32)
        for k in range(1, nd):
            total = total + cgr[c, k - 1].astype(f32)
        penalty = sparsity_weight * loss_scale * (sq[1, 0:1, :] + sq[2, 0:1, :])
        pg[c, my_rows, :] = ((total + penalty) * 2.0 * act[c]).astype(bf16)
        for k in range(1, nd):
            block = pg.at[c, my_rows]
            pg_copies[c, k] = go(remote(block, block, pg_s.at[c, k - 1], pg_r.at[c, k - 1], dpeer[k]))

    outs = []

    def finish(c):
        for k in range(1, nd):
            pg_copies[c, k].wait_recv()
        copy = pltpu.make_async_copy(pg.at[c], pg_out.at[c], out_sem.at[c])
        copy.start()
        outs.append(copy)

    forward(0)
    dec_copies = []
    for h in range(feats // lats):
        copy = pltpu.make_async_copy(
            dec_w.at[:, pl.ds(h * lats, lats)], stage.at[pl.ds(h * lats, lats)], local_sem.at[3 + h]
        )
        copy.start()
        dec_copies.append(copy)
    for copy in dec_copies:
        copy.wait()

    @pl.loop(0, lats // 128)
    def _(i):
        acc = jnp.zeros((128, 128), f32)
        r = pl.ds(pl.multiple_of(i * 128, 128), 128)
        for h in range(feats // lats):
            x = stage[pl.ds(pl.multiple_of(h * lats + i * 128, 128), 128), :]
            dec16[r, pl.ds(h * lats, lats)] = x.astype(bf16)
            for q in range(lats // 128):
                y = x[:, q * 128:(q + 1) * 128]
                acc = acc + y * y
        line = jnp.sum(acc.T, axis=0, keepdims=True)
        sq[0, :, r] = jnp.broadcast_to(line, (8, 128))

    sq_copies = [
        go(remote(sq.at[0], sqr.at[k - 1], sq_s.at[k - 1], sq_r.at[k - 1], dpeer[k]))
        for k in range(1, nd)
    ]

    def norms():
        for copy in sq_copies:
            copy.wait_recv()
        mine = sq[0]
        first = jnp.where(me < nd // 2, mine, 0.0)
        second = mine - first
        for k in range(1, nd):
            x = sqr[k - 1]
            low = jnp.where(behind[k] < nd // 2, x, 0.0)
            first, second = first + low, second + (x - low)
        sq[1] = jnp.sqrt(first + norm_eps)
        sq[2] = jnp.sqrt(second + norm_eps)
        copy = pltpu.make_async_copy(sq.at[pl.ds(1, 2)], norms_out, local_sem.at[1])
        copy.start()
        outs.append(copy)

    bf_copies = []

    def send_buffer():
        for k in range(1, nd):
            bf_copies.append(go(remote(
                outgoing.at[ahead[k]], arrived.at[me], bf_s.at[k - 1], bf_r.at[k - 1], dpeer[k]
            )))

    def put(ref, out, base, c):
        copy = pltpu.make_async_copy(ref.at[c], out.at[c], out_sem.at[base * chunks + c])
        copy.start()
        outs.append(copy)

    steps = [forward, encode, activate, decode]
    steps += [functools.partial(halve, b) for b in range(nb)]
    steps += [error]
    steps += [functools.partial(widen, b) for b in reversed(range(nb - 1))]
    steps += [share, back, grad, finish]
    lead = 1
    for t in range(len(steps) + lead * (chunks - 1)):
        for c in range(chunks):
            s = t - lead * c
            if 0 <= s < len(steps) and not (s == 0 and c == 0):
                steps[s](c)
                if s == 3:
                    put(col, col_out, 1, c)
                    put(codes, codes_out, 2, c)
                if steps[s] is back:
                    put(err, err_out, 3, c)
                if s == 2 and c == chunks - 1:
                    send_buffer()
                if s == 4 and c == 0:
                    norms()
    for copy in bf_copies:
        copy.wait_recv()
    own_block.wait()
    for copy in outs:
        copy.wait()
    for copy in sends:
        copy.wait_send()


def exchange(nd, nl, paired, enc_weight, dec_weight, enc_bias, dec_bias, outgoing):
    chunks = CHUNKS
    rows = paired.shape[0] // chunks
    feats, lats = enc_weight.shape
    m = rows * nd
    nb = rounds_of(nl)
    bf16, f32 = jnp.bfloat16, jnp.float32
    hbm = pl.BlockSpec(memory_space=pl.ANY)
    vmem = pl.BlockSpec(memory_space=pltpu.VMEM)
    dma = pltpu.SemaphoreType.DMA
    peers = nd - 1
    big = [(chunks, m, feats), (chunks, m, lats)]
    pair = [dma((chunks, peers)), dma((chunks, peers))]
    single = [dma((chunks,)), dma((chunks,))]
    zs = [dma((chunks, nb)), dma((chunks, nb))]
    flops = 3 * 2 * chunks * m * feats * lats
    return pl.pallas_call(
        functools.partial(kernel, nd, nl, chunks),
        out_shape=(
            jax.ShapeDtypeStruct(big[0], bf16),
            jax.ShapeDtypeStruct(big[1], bf16),
            jax.ShapeDtypeStruct(big[0], bf16),
            jax.ShapeDtypeStruct(big[1], bf16),
            jax.ShapeDtypeStruct((2, 8, lats), f32),
            jax.ShapeDtypeStruct(outgoing.shape, bf16),
        ),
        in_specs=[hbm, hbm, hbm, vmem, vmem, hbm],
        out_specs=(hbm,) * 6,
        scratch_shapes=[
            pltpu.VMEM(big[0], bf16),
            pltpu.VMEM((feats, lats), bf16),
            pltpu.VMEM((lats, feats), bf16),
            pltpu.VMEM((feats, lats), f32),
            pltpu.VMEM(big[1], bf16),
            pltpu.VMEM((chunks, peers, rows, lats), bf16),
            pltpu.VMEM((chunks, rows, lats), f32),
            pltpu.VMEM(big[1], bf16),
            pltpu.VMEM(big[0], bf16),
            pltpu.VMEM((chunks, m // 2, feats), bf16),
            pltpu.VMEM((chunks, m // 2, feats), bf16),
            pltpu.VMEM(big[0], bf16),
            pltpu.VMEM(big[1], bf16),
            pltpu.VMEM((chunks, peers, rows, lats), bf16),
            pltpu.VMEM(big[1], bf16),
            pltpu.VMEM((3, 8, lats), f32),
            pltpu.VMEM((peers, 8, lats), f32),
            dma((8,)),
            *pair, *pair, *pair, *pair, *single, *zs, *zs, *single, *pair, *pair,
            dma((peers,)), dma((peers,)), dma((peers,)), dma((peers,)),
            dma((chunks,)), dma((4 * chunks,)),
        ],
        compiler_params=pltpu.CompilerParams(
            collective_id=0, has_side_effects=True, vmem_limit_bytes=60 * 1024 * 1024
        ),
        cost_estimate=pl.CostEstimate(flops=flops, bytes_accessed=40 << 20, transcendentals=0),
    )(paired, enc_weight, dec_weight, enc_bias[None, :], dec_bias[None, :], outgoing)


def body(paired, enc_weight, enc_bias, dec_weight, dec_bias, buffer_rows, block_dest):
    data_count = lax.axis_size("dp")
    latent_count = lax.axis_size("latent")
    data_index = lax.axis_index("dp")
    contract_rows = (((0,), (0,)), ((), ()))
    blocks_here = buffer_rows.shape[0] // BLOCK_ROWS
    per_device = blocks_here // data_count
    block_iota = jnp.arange(blocks_here, dtype=jnp.int32)
    own_dest = lax.dynamic_slice_in_dim(block_dest, data_index * blocks_here, blocks_here, 0)
    target_device = own_dest // blocks_here
    earlier_same = (target_device[None, :] == target_device[:, None]) & (
        own_dest[None, :] < own_dest[:, None]
    )
    send_slot = target_device * per_device + jnp.sum(earlier_same.astype(jnp.int32), axis=1)
    chosen = jnp.sum(
        jnp.where(send_slot[None, :] == block_iota[:, None], block_iota[None, :], 0), axis=1
    )
    feature_count = buffer_rows.shape[1]
    outgoing = buffer_rows.reshape(blocks_here, BLOCK_ROWS, feature_count)[chosen].reshape(
        data_count, buffer_rows.shape[0] // data_count, feature_count
    )
    col, codes, err, pg, norms, arrived = exchange(
        data_count, latent_count, paired, enc_weight, dec_weight, enc_bias, dec_bias, outgoing
    )
    feats, lats = enc_weight.shape
    col, err = col.reshape(-1, feats), err.reshape(-1, feats)
    codes, pg = codes.reshape(-1, lats), pg.reshape(-1, lats)
    enc_grad = lax.dot_general(col, pg, contract_rows, preferred_element_type=jnp.float32)
    model_index = data_index // (data_count // 2)
    own_norm = jnp.where(model_index == 0, norms[0, 0], norms[1, 0])
    code_sum = jnp.sum(codes, axis=0, dtype=jnp.float32)
    dec_main = lax.dot_general(codes, err, contract_rows, preferred_element_type=jnp.float32)
    dec_grad = (
        dec_main + sparsity_weight * loss_scale * code_sum[:, None] * dec_weight / own_norm[:, None]
    )
    positions = data_index * blocks_here + block_iota
    every_block = jnp.arange(block_dest.shape[0], dtype=jnp.int32)
    source_block = jnp.sum(
        jnp.where(block_dest[None, :] == positions[:, None], every_block[None, :], 0), axis=1
    )
    sender_device = source_block // blocks_here
    before_same = (sender_device[None, :] == sender_device[:, None]) & (
        block_iota[None, :] < block_iota[:, None]
    )
    arrival_slot = sender_device * per_device + jnp.sum(before_same.astype(jnp.int32), axis=1)
    shuffled = arrived.reshape(blocks_here, BLOCK_ROWS, feature_count)[arrival_slot].reshape(
        buffer_rows.shape
    )
    return (enc_grad, dec_grad, shuffled)


def solution(mesh):
    in_specs = (
        P("dp", None),
        P("dp", "latent"),
        P("latent"),
        P("latent", "dp"),
        P("dp"),
        P("dp", "latent"),
        P(),
    )
    out_specs = (P("dp", "latent"), P("latent", "dp"), P("dp", "latent"))
    return jax.shard_map(body, mesh=mesh, in_specs=in_specs, out_specs=out_specs, check_vma=False)
```

```python
import functools

import jax
import jax.numpy as jnp
from jax import lax
from jax.experimental import pallas as pl
from jax.experimental.pallas import tpu as pltpu
from jax.sharding import PartitionSpec as P

BLOCK_ROWS = 64
CHUNKS = 4
TILE = 256
MESH = pl.DeviceIdType.MESH

loss_scale = 0.03125
sparsity_weight = 4.0
norm_eps = 1e-06


def rounds_of(latent_count):
    return (latent_count // 2).bit_length() - 1


def kernel(
    nd, nl, chunks,
    paired, enc_w, dec_w, enc_b, dec_b, outgoing,
    col_out, pg_out, dec_out, arrived,
    col, enc16, dec16, stage, part, prec, act, codes, rp, crx, zrx, err, cgp, cgr, pg, sq, sqr, codest, scale, dtile,
    local_sem, pair_s, pair_r, fwd_s, fwd_r, pp_s, pp_r, cd_s, cd_r, cx_s, cx_r, zx_s, zx_r,
    za_s, za_r, ca_s, ca_r, cg_s, cg_r, pg_s, pg_r, sq_s, sq_r, bf_s, bf_r, own_sem, out_sem, tile_sem,
):
    f32, bf16 = jnp.float32, jnp.bfloat16
    rows = paired.shape[0] // chunks
    feats, lats = enc_w.shape
    m = rows * nd
    half = feats // 2
    nb = rounds_of(nl)
    me = lax.axis_index("dp")
    li = lax.axis_index("latent")
    zi = lax.div(li, 2)
    core = lax.rem(li, 2)
    mate = {"latent": li + 1 - 2 * core}
    bits = [lax.rem(lax.div(zi, 1 << b), 2) for b in range(nb)]
    zpeer = [{"latent": li + (2 << b) * (1 - 2 * bits[b])} for b in range(nb)]
    ahead = [lax.rem(me + k, nd) for k in range(nd)]
    behind = [lax.rem(me + nd - k, nd) for k in range(nd)]
    dpeer = [{"dp": ahead[k]} for k in range(nd)]

    def at_rows(index, size):
        return pl.ds(pl.multiple_of(index, 16), size)

    my_rows = at_rows(me * rows, rows)

    def remote(src, dst, s, r, dev):
        return pltpu.make_async_remote_copy(
            src_ref=src, dst_ref=dst, send_sem=s, recv_sem=r, device_id=dev, device_id_type=MESH
        )

    enc_copy = pltpu.make_async_copy(enc_w, stage, local_sem.at[0])
    enc_copy.start()

    barrier = pltpu.get_barrier_semaphore()
    friends = dpeer[1:] + [mate] + zpeer
    for dev in friends:
        pl.semaphore_signal(barrier, inc=1, device_id=dev, device_id_type=MESH)
    pl.semaphore_wait(barrier, len(friends))

    sends = []

    def go(copy):
        copy.start()
        sends.append(copy)
        return copy

    my_half = pl.ds(pl.multiple_of(core * half, 128), half)
    pair_copies, fwd_copies, own_copies = {}, {}, {}
    def send_pair(c):
        for k in range(1, nd):
            source = pl.ds(pl.multiple_of(ahead[k] * feats + core * half, 128), half)
            pair_copies[c, k] = go(remote(
                paired.at[pl.ds(c * rows, rows), source],
                col.at[c, my_rows, my_half],
                pair_s.at[c, k - 1], pair_r.at[c, k - 1], dpeer[k],
            ))
        own_copies[c] = pltpu.make_async_copy(
            paired.at[pl.ds(c * rows, rows), pl.ds(pl.multiple_of(me * feats, 128), feats)],
            col.at[c, my_rows],
            own_sem.at[c],
        )
        own_copies[c].start()

    for c in range(1):
        send_pair(c)
    own_block = pltpu.make_async_copy(outgoing.at[me], arrived.at[me], local_sem.at[2])
    own_block.start()

    enc_copy.wait()

    @pl.loop(0, feats // 128)
    def _(i):
        r = pl.ds(pl.multiple_of(i * 128, 128), 128)
        enc16[r, :] = stage[r, :].astype(bf16)

    def forward(c):
        for k in range(1, nd):
            pair_copies[c, k].wait_recv()
            block = col.at[c, at_rows(behind[k] * rows, rows), my_half]
            fwd_copies[c, k] = go(remote(block, block, fwd_s.at[c, k - 1], fwd_r.at[c, k - 1], mate))

    pp_copies, cd_copies, cx_copies, zx_copies = {}, {}, {}, {}
    za_copies, ca_copies, cg_copies, pg_copies = {}, {}, {}, {}

    def encode(c):
        own_copies[c].wait()
        for k in range(1, nd):
            fwd_copies[c, k].wait_recv()

        @pl.loop(0, lats // TILE)
        def _(j):
            t = pl.ds(pl.multiple_of(j * TILE, TILE), TILE)
            part[c, :, t] = jnp.dot(col[c], enc16[:, t], preferred_element_type=f32).astype(bf16)

        for k in range(1, nd):
            pp_copies[c, k] = go(remote(
                part.at[c, at_rows(ahead[k] * rows, rows)], prec.at[c, k - 1],
                pp_s.at[c, k - 1], pp_r.at[c, k - 1], dpeer[k],
            ))

    def activate(c):
        for k in range(1, nd):
            pp_copies[c, k].wait_recv()
        total = part[c, my_rows, :].astype(f32)
        for k in range(1, nd):
            total = total + prec[c, k - 1].astype(f32)
        a = jnp.maximum(total + enc_b[...], 0.0)
        act[c] = a
        codes[c, my_rows, :] = (a * a).astype(bf16)
        for k in range(1, nd):
            block = codes.at[c, my_rows]
            cd_copies[c, k] = go(remote(block, block, cd_s.at[c, k - 1], cd_r.at[c, k - 1], dpeer[k]))

    def decode(c):
        for k in range(1, nd):
            cd_copies[c, k].wait_recv()

        @pl.loop(0, feats // TILE)
        def _(j):
            t = pl.ds(pl.multiple_of(j * TILE, TILE), TILE)
            rp[c, :, t] = jnp.dot(codes[c], dec16[:, t], preferred_element_type=f32).astype(bf16)

        cx_copies[c] = go(remote(
            rp.at[c, at_rows((1 - core) * (m // 2), m // 2)], crx.at[c], cx_s.at[c], cx_r.at[c], mate
        ))

        @pl.loop(0, lats // TILE)
        def _(j):
            t = pl.ds(pl.multiple_of(j * TILE, TILE), TILE)
            codest[t, pl.ds(c * m, m)] = codes[c, :, t].T

    bases, sizes = [core * (m // 2)], [m // 2]
    for b in range(nb):
        sizes.append(sizes[-1] // 2)
        bases.append(bases[-1] + bits[b] * sizes[-1])
    zoff = [0]
    for b in range(nb):
        zoff.append(zoff[-1] + sizes[b + 1])

    def add_rows(c, base, size, source, start):
        @pl.loop(0, size // 32)
        def _(i):
            r = at_rows(base + i * 32, 32)
            s = at_rows(start + i * 32, 32)
            rp[c, r, :] = (rp[c, r, :].astype(f32) + source[c, s, :].astype(f32)).astype(bf16)

    def halve(b, c):
        if b == 0:
            cx_copies[c].wait_recv()
            add_rows(c, bases[0], sizes[0], crx, 0)
        else:
            zx_copies[c, b - 1].wait_recv()
            add_rows(c, bases[b], sizes[b], zrx, zoff[b - 1])
        size = sizes[b + 1]
        zx_copies[c, b] = go(remote(
            rp.at[c, at_rows(bases[b] + (1 - bits[b]) * size, size)],
            zrx.at[c, pl.ds(zoff[b], size)],
            zx_s.at[c, b], zx_r.at[c, b], zpeer[b],
        ))

    def spread(b, c):
        block = err.at[c, at_rows(bases[b + 1], sizes[b + 1])]
        za_copies[c, b] = go(remote(block, block, za_s.at[c, b], za_r.at[c, b], zpeer[b]))

    def error(c):
        b = nb - 1
        zx_copies[c, b].wait_recv()

        @pl.loop(0, sizes[nb] // 32)
        def _(i):
            r = at_rows(bases[nb] + i * 32, 32)
            s = at_rows(zoff[b] + i * 32, 32)
            recon = rp[c, r, :].astype(f32) + zrx[c, s, :].astype(f32) + dec_b[...]
            err[c, r, :] = (2.0 * loss_scale * (recon - col[c, r, :].astype(f32))).astype(bf16)

        spread(b, c)

    def widen(b, c):
        za_copies[c, b + 1].wait_recv()
        spread(b, c)

    def share(c):
        za_copies[c, 0].wait_recv()
        block = err.at[c, at_rows(bases[0], m // 2)]
        ca_copies[c] = go(remote(block, block, ca_s.at[c], ca_r.at[c], mate))

    def back(c):
        ca_copies[c].wait_recv()

        @pl.loop(0, lats // TILE)
        def _(j):
            t = pl.ds(pl.multiple_of(j * TILE, TILE), TILE)
            cgp[c, :, t] = lax.dot_general(
                err[c], dec16[t, :], (((1,), (1,)), ((), ())), preferred_element_type=f32
            ).astype(bf16)

        for k in range(1, nd):
            cg_copies[c, k] = go(remote(
                cgp.at[c, at_rows(ahead[k] * rows, rows)], cgr.at[c, k - 1],
                cg_s.at[c, k - 1], cg_r.at[c, k - 1], dpeer[k],
            ))

    def grad(c):
        for k in range(1, nd):
            cg_copies[c, k].wait_recv()
        total = cgp[c, my_rows, :].astype(f32)
        for k in range(1, nd):
            total = total + cgr[c, k - 1].astype(f32)
        penalty = sparsity_weight * loss_scale * (sq[1, 0:1, :] + sq[2, 0:1, :])
        pg[c, my_rows, :] = ((total + penalty) * 2.0 * act[c]).astype(bf16)
        for k in range(1, nd):
            block = pg.at[c, my_rows]
            pg_copies[c, k] = go(remote(block, block, pg_s.at[c, k - 1], pg_r.at[c, k - 1], dpeer[k]))

    outs = []

    def finish(c):
        for k in range(1, nd):
            pg_copies[c, k].wait_recv()
        copy = pltpu.make_async_copy(pg.at[c], pg_out.at[c], out_sem.at[c])
        copy.start()
        outs.append(copy)

    forward(0)
    dec_copies = []
    for h in range(feats // lats):
        copy = pltpu.make_async_copy(
            dec_w.at[:, pl.ds(h * lats, lats)], stage.at[pl.ds(h * lats, lats)], local_sem.at[3 + h]
        )
        copy.start()
        dec_copies.append(copy)
    for copy in dec_copies:
        copy.wait()

    @pl.loop(0, lats // 128)
    def _(i):
        acc = jnp.zeros((128, 128), f32)
        r = pl.ds(pl.multiple_of(i * 128, 128), 128)
        for h in range(feats // lats):
            x = stage[pl.ds(pl.multiple_of(h * lats + i * 128, 128), 128), :]
            dec16[r, pl.ds(h * lats, lats)] = x.astype(bf16)
            for q in range(lats // 128):
                y = x[:, q * 128:(q + 1) * 128]
                acc = acc + y * y
        line = jnp.sum(acc.T, axis=0, keepdims=True)
        sq[0, :, r] = jnp.broadcast_to(line, (8, 128))

    sq_copies = [
        go(remote(sq.at[0], sqr.at[k - 1], sq_s.at[k - 1], sq_r.at[k - 1], dpeer[k]))
        for k in range(1, nd)
    ]

    def norms():
        for copy in sq_copies:
            copy.wait_recv()
        mine = sq[0]
        first = jnp.where(me < nd // 2, mine, 0.0)
        second = mine - first
        for k in range(1, nd):
            x = sqr[k - 1]
            low = jnp.where(behind[k] < nd // 2, x, 0.0)
            first, second = first + low, second + (x - low)
        sq[1] = jnp.sqrt(first + norm_eps)
        sq[2] = jnp.sqrt(second + norm_eps)

    def scales():
        @pl.loop(0, lats // 128)
        def _(i):
            r = pl.ds(pl.multiple_of(i * 128, 128), 128)
            total = jnp.sum(codest[r, :].astype(f32), axis=1, keepdims=True)
            norm = jnp.where(me < nd // 2, sq[1, 0:1, r], sq[2, 0:1, r])
            spread_norm = jnp.broadcast_to(norm, (128, 128)).T
            scale[r, :] = sparsity_weight * loss_scale * total / spread_norm

    tiles = []

    def dec_tile(j):
        slot = j % 2
        if j >= 2:
            tiles[j - 2].wait()
        start = (j * TILE // lats) * lats
        lane = j * TILE % lats

        @pl.loop(0, lats // 256)
        def _(i):
            r = pl.ds(pl.multiple_of(i * 256, 256), 256)
            w = pl.ds(pl.multiple_of(start + i * 256, 256), 256)
            acc = jnp.zeros((256, TILE), f32)
            for c in range(chunks):
                acc = acc + jnp.dot(
                    codest[r, c * m:(c + 1) * m], err[c, :, j * TILE:(j + 1) * TILE],
                    preferred_element_type=f32,
                )
            for q in range(TILE // 128):
                dtile[slot, r, q * 128:(q + 1) * 128] = (
                    acc[:, q * 128:(q + 1) * 128]
                    + scale[r, :] * stage[w, lane + q * 128:lane + (q + 1) * 128]
                )

        copy = pltpu.make_async_copy(
            dtile.at[slot], dec_out.at[:, pl.ds(j * TILE, TILE)], tile_sem.at[slot]
        )
        copy.start()
        tiles.append(copy)

    bf_copies = []

    def send_buffer():
        for k in range(1, nd):
            bf_copies.append(go(remote(
                outgoing.at[ahead[k]], arrived.at[me], bf_s.at[k - 1], bf_r.at[k - 1], dpeer[k]
            )))

    def put(ref, out, base, c):
        copy = pltpu.make_async_copy(ref.at[c], out.at[c], out_sem.at[base * chunks + c])
        copy.start()
        outs.append(copy)

    steps = [forward, encode, activate, decode]
    steps += [functools.partial(halve, b) for b in range(nb)]
    steps += [error]
    steps += [functools.partial(widen, b) for b in reversed(range(nb - 1))]
    steps += [share, back, grad, finish]
    lead = 2
    count = feats // TILE
    sent = [1]
    for t in range(len(steps) + lead * (chunks - 1)):
        while sent[0] < chunks and t >= lead * sent[0] - 2:
            send_pair(sent[0])
            sent[0] += 1
        for c in reversed(range(chunks)):
            s = t - lead * c
            if 0 <= s < len(steps) and not (s == 0 and c == 0):
                steps[s](c)
                if s == 3:
                    put(col, col_out, 1, c)
                    if c == chunks - 1:
                        scales()
                if s == 2 and c == chunks - 1:
                    send_buffer()
                if s == 2 and c == 1:
                    norms()
                if c == chunks - 1 and steps[s] is back:
                    for j in range(count // 2):
                        dec_tile(j)
                if c == chunks - 1 and steps[s] is grad:
                    for j in range(count // 2, count):
                        dec_tile(j)
    for copy in bf_copies:
        copy.wait_recv()
    own_block.wait()
    for copy in tiles[-2:]:
        copy.wait()
    for copy in outs:
        copy.wait()
    for copy in sends:
        copy.wait_send()


def exchange(nd, nl, paired, enc_weight, dec_weight, enc_bias, dec_bias, outgoing):
    chunks = CHUNKS
    rows = paired.shape[0] // chunks
    feats, lats = enc_weight.shape
    m = rows * nd
    nb = rounds_of(nl)
    bf16, f32 = jnp.bfloat16, jnp.float32
    hbm = pl.BlockSpec(memory_space=pl.ANY)
    vmem = pl.BlockSpec(memory_space=pltpu.VMEM)
    dma = pltpu.SemaphoreType.DMA
    peers = nd - 1
    big = [(chunks, m, feats), (chunks, m, lats)]
    pair = [dma((chunks, peers)), dma((chunks, peers))]
    single = [dma((chunks,)), dma((chunks,))]
    zs = [dma((chunks, nb)), dma((chunks, nb))]
    flops = 3 * 2 * chunks * m * feats * lats
    return pl.pallas_call(
        functools.partial(kernel, nd, nl, chunks),
        out_shape=(
            jax.ShapeDtypeStruct(big[0], bf16),
            jax.ShapeDtypeStruct(big[1], bf16),
            jax.ShapeDtypeStruct((lats, feats), f32),
            jax.ShapeDtypeStruct(outgoing.shape, bf16),
        ),
        in_specs=[hbm, hbm, hbm, vmem, vmem, hbm],
        out_specs=(hbm,) * 4,
        scratch_shapes=[
            pltpu.VMEM(big[0], bf16),
            pltpu.VMEM((feats, lats), bf16),
            pltpu.VMEM((lats, feats), bf16),
            pltpu.VMEM((feats, lats), f32),
            pltpu.VMEM(big[1], bf16),
            pltpu.VMEM((chunks, peers, rows, lats), bf16),
            pltpu.VMEM((chunks, rows, lats), f32),
            pltpu.VMEM(big[1], bf16),
            pltpu.VMEM(big[0], bf16),
            pltpu.VMEM((chunks, m // 2, feats), bf16),
            pltpu.VMEM((chunks, m // 2, feats), bf16),
            pltpu.VMEM(big[0], bf16),
            pltpu.VMEM(big[1], bf16),
            pltpu.VMEM((chunks, peers, rows, lats), bf16),
            pltpu.VMEM(big[1], bf16),
            pltpu.VMEM((3, 8, lats), f32),
            pltpu.VMEM((peers, 8, lats), f32),
            pltpu.VMEM((lats, chunks * m), bf16),
            pltpu.VMEM((lats, 128), f32),
            pltpu.VMEM((2, lats, TILE), f32),
            dma((8,)),
            *pair, *pair, *pair, *pair, *single, *zs, *zs, *single, *pair, *pair,
            dma((peers,)), dma((peers,)), dma((peers,)), dma((peers,)),
            dma((chunks,)), dma((2 * chunks,)), dma((2,)),
        ],
        compiler_params=pltpu.CompilerParams(
            collective_id=0, has_side_effects=True, vmem_limit_bytes=60 * 1024 * 1024
        ),
        cost_estimate=pl.CostEstimate(flops=flops, bytes_accessed=40 << 20, transcendentals=0),
    )(paired, enc_weight, dec_weight, enc_bias[None, :], dec_bias[None, :], outgoing)


def body(paired, enc_weight, enc_bias, dec_weight, dec_bias, buffer_rows, block_dest):
    data_count = lax.axis_size("dp")
    latent_count = lax.axis_size("latent")
    data_index = lax.axis_index("dp")
    contract_rows = (((0,), (0,)), ((), ()))
    blocks_here = buffer_rows.shape[0] // BLOCK_ROWS
    per_device = blocks_here // data_count
    block_iota = jnp.arange(blocks_here, dtype=jnp.int32)
    own_dest = lax.dynamic_slice_in_dim(block_dest, data_index * blocks_here, blocks_here, 0)
    target_device = own_dest // blocks_here
    earlier_same = (target_device[None, :] == target_device[:, None]) & (
        own_dest[None, :] < own_dest[:, None]
    )
    send_slot = target_device * per_device + jnp.sum(earlier_same.astype(jnp.int32), axis=1)
    chosen = jnp.sum(
        jnp.where(send_slot[None, :] == block_iota[:, None], block_iota[None, :], 0), axis=1
    )
    feature_count = buffer_rows.shape[1]
    outgoing = buffer_rows.reshape(blocks_here, BLOCK_ROWS, feature_count)[chosen].reshape(
        data_count, buffer_rows.shape[0] // data_count, feature_count
    )
    col, pg, dec_grad, arrived = exchange(
        data_count, latent_count, paired, enc_weight, dec_weight, enc_bias, dec_bias, outgoing
    )
    feats, lats = enc_weight.shape
    enc_grad = lax.dot_general(
        col.reshape(-1, feats), pg.reshape(-1, lats), contract_rows,
        preferred_element_type=jnp.float32,
    )
    positions = data_index * blocks_here + block_iota
    every_block = jnp.arange(block_dest.shape[0], dtype=jnp.int32)
    source_block = jnp.sum(
        jnp.where(block_dest[None, :] == positions[:, None], every_block[None, :], 0), axis=1
    )
    sender_device = source_block // blocks_here
    before_same = (sender_device[None, :] == sender_device[:, None]) & (
        block_iota[None, :] < block_iota[:, None]
    )
    arrival_slot = sender_device * per_device + jnp.sum(before_same.astype(jnp.int32), axis=1)
    shuffled = arrived.reshape(blocks_here, BLOCK_ROWS, feature_count)[arrival_slot].reshape(
        buffer_rows.shape
    )
    return (enc_grad, dec_grad, shuffled)


def solution(mesh):
    in_specs = (
        P("dp", None),
        P("dp", "latent"),
        P("latent"),
        P("latent", "dp"),
        P("dp"),
        P("dp", "latent"),
        P(),
    )
    out_specs = (P("dp", "latent"), P("latent", "dp"), P("dp", "latent"))
    return jax.shard_map(body, mesh=mesh, in_specs=in_specs, out_specs=out_specs, check_vma=False)
```
